32 devices in a mesh: parts: 2 (over y), row: 4 (over z), col: 2 (over x), head: 2 (over core).
Axes of the slice: x: 2, y: 2, z: 4, core: 2. Of those that a mesh axis runs over, the one named last changes fastest.
Arguments:
- pair: bfloat16 [1536, 768, 128], P(('parts', 'row'), 'col'), parts along dimension 0, may hold values from -20 to 20
- crop_length: int32 [2], P('parts'), parts along dimension 0, may hold values from 576 to 768, as said below
- residue_mask: int32 [1536], P('parts'), parts along dimension 0, may hold values from 0 to 1, as said below
- ln_gain: float32 [128], replicated, may hold values from 0.1 to 1.9
- w_query: bfloat16 [128, 128], P(None, 'head'), may hold values from -1 to 1
- w_key: bfloat16 [128, 128], P(None, 'head'), may hold values from -8 to 8
- w_value: bfloat16 [128, 128], P(None, 'head'), may hold values from -0.5 to 0.5
- w_gate: bfloat16 [128, 128], P(None, 'head'), may hold values from -0.5 to 0.5
- gate_bias: float32 [128], P('head'), may hold values from -4 to 4
- w_bias: bfloat16 [128, 4], P(None, 'head'), may hold values from -0.5 to 0.5
- w_out: bfloat16 [128, 128], replicated, may hold values from -1.5 to 1.5
Outputs:
- update: bfloat16 [1536, 768, 128], P(('parts', 'row'), ('col', 'head')), parts along dimension 0
The draws below stay inside these ranges and needn't reach their ends.
There are 2 independent parts, one for each index of `parts`. The reference program is written for one: setup_inputs(seed, part) draws one part's arguments, and reference() takes and returns one part's arrays. A program takes and returns all parts, laid end to end along the dimension named above; an argument that names none is the same for every part. Nothing has to cross between parts.
Inputs may be any that keep to these rules, and one draw needn't show every extreme that they name: `crop_length`: in every odd group the crop fills the whole grid; in every even group it is shorter. `residue_mask`: the first residue is 1.
All inputs are finite; a program needn't handle non-finite values.
Results may differ from the reference program's by a relative error of at most 0.012.
The reference program's roundings to bfloat16 on the way (of `normed`, `query`, `bias`, `weights` and `gated`) count: a program that leaves them out, or rounds other values in their place, can miss the bound.
Values may be sent and summed in bfloat16 or wider, within the bound.
A program may use at most 256 MiB of HBM per device.

```python
import math
import jax
import jax.numpy as jnp
from jax import lax

C = 128
HEADS = 4
HEAD_DIM = 32
GRID = 768
HD = 128


def shared_query(key):
    base = jax.random.normal(jax.random.fold_in(key, 103), (C, HD), jnp.float32)
    return jnp.clip(base, -4.0, 4.0) / math.sqrt(C)


def draw_crop_length(key, part):
    key = jax.random.fold_in(key, 7)
    shorter = jax.random.randint(key, (), 1, GRID // 4 + 1)
    found = GRID - (1 - part % 2) * shorter
    return jnp.reshape(found, (1,)).astype(jnp.int32)


def draw_residue_mask(key, part):
    key = jax.random.fold_in(key, 8)
    resolved = (jax.random.randint(key, (GRID,), 0, 10) < 9).astype(jnp.int32)
    ids = jnp.arange(GRID, dtype=jnp.int32)
    return jnp.where(ids == 0, 1, resolved).astype(jnp.int32)


def draw_w_query(key, part):
    shared = shared_query(key)
    return shared.astype(jnp.bfloat16)


def draw_w_key(key, part):
    key = jax.random.fold_in(key, 12)
    own = jnp.clip(jax.random.normal(key, (C, HD), jnp.float32), -4.0, 4.0) / math.sqrt(C)
    return own.astype(jnp.bfloat16)


def draw_pair(key, part):
    key = jax.random.fold_in(key, 1)
    first_key = jax.random.fold_in(key, 0)
    base = jnp.clip(jax.random.normal(first_key, (GRID, GRID, C), jnp.float32), -6.0, 6.0)
    return base.astype(jnp.bfloat16)


def level_of(stream_key, shape, pieces, least, top_value):
    level, own = 1.0, jax.random.fold_in(stream_key, 6)
    for dim, blocks in pieces:
        steps = jnp.exp(jax.random.uniform(jax.random.fold_in(own, dim), (blocks,), jnp.float32, least / len(pieces), top_value / len(pieces)))
        level = level * jnp.repeat(steps, shape[dim] // blocks).reshape([-1 if axis == dim else 1 for axis in range(len(shape))])
    return level


def scatter_about(stream_key, shape, width, most, cuts=(), held_as=jnp.bfloat16):
    array = jax.random.normal(stream_key, shape, jnp.float32) * width
    if len(cuts) > 0:
        array = level_of(stream_key, shape, cuts, -0.22, 0.18) * array
    return jnp.clip(array, min=-most, max=most).astype(held_as)


def setup_inputs(seed: int = 0, part: int = 0) -> dict:
    key_of = jax.random.split(jax.random.key(seed), 12)
    own_keys = jax.random.split(jax.random.fold_in(key_of[11], part), 12)
    pair = draw_pair(jax.random.fold_in(jax.random.fold_in(key_of[11], part), 71), part)
    crop_length = draw_crop_length(jax.random.fold_in(jax.random.fold_in(key_of[11], part), 71), part)
    residue_mask = draw_residue_mask(jax.random.fold_in(jax.random.fold_in(key_of[11], part), 71), part)
    ln_gain = jnp.clip(1.0 + 0.18 * jax.random.normal(key_of[3], (C,), jnp.float32), 0.1, 1.9)
    w_query = draw_w_query(jax.random.fold_in(key_of[11], 71), part)
    w_key = draw_w_key(jax.random.fold_in(key_of[11], 71), part)
    w_value = scatter_about(key_of[6], (C, HD), C ** -0.5, 0.5, ((1, 2),))
    w_gate = scatter_about(key_of[7], (C, HD), C ** -0.5, 0.5, ((1, 2),))
    gate_bias = scatter_about(key_of[8], (HD,), 1.0, 4.0, ((0, 2),), jnp.float32)
    w_bias = scatter_about(key_of[9], (C, HEADS), C ** -0.5, 0.5, ((1, 2),))
    w_out = scatter_about(key_of[10], (HD, C), 0.25, 1.5)
    return {"pair": pair, "crop_length": crop_length, "residue_mask": residue_mask, "ln_gain": ln_gain, "w_query": w_query, "w_key": w_key, "w_value": w_value, "w_gate": w_gate, "gate_bias": gate_bias, "w_bias": w_bias, "w_out": w_out}


def layer_norm(pair, ln_gain):
    values = pair.astype(jnp.float32)
    centre = values - lax.optimization_barrier(jnp.mean(values, axis=-1, keepdims=True))
    spread = lax.optimization_barrier(jnp.mean(centre * centre, axis=-1, keepdims=True))
    return (centre * lax.rsqrt(spread + 1e-05) * ln_gain).astype(jnp.bfloat16)

def reference(pair, crop_length, residue_mask, ln_gain, w_query, w_key, w_value, w_gate, gate_bias, w_bias, w_out):
    normed = layer_norm(pair, ln_gain)
    flat = normed.reshape(GRID * GRID, C)
    scale = 1.0 / HEAD_DIM ** 0.5
    query = (jnp.dot(flat, w_query, preferred_element_type=jnp.float32) * scale).astype(jnp.bfloat16)
    keys = jnp.dot(flat, w_key, preferred_element_type=jnp.float32).astype(jnp.bfloat16)
    values = jnp.dot(flat, w_value, preferred_element_type=jnp.float32).astype(jnp.bfloat16)
    gate = jax.nn.sigmoid(jnp.dot(flat, w_gate, preferred_element_type=jnp.float32) + gate_bias)
    bias = jnp.dot(flat, w_bias, preferred_element_type=jnp.float32).astype(jnp.bfloat16)
    bias = jnp.transpose(bias.reshape(GRID, GRID, HEADS), (2, 0, 1)).astype(jnp.float32)
    total_len = crop_length[0]
    key_ids = jnp.arange(GRID, dtype=jnp.int32)
    key_live = (residue_mask == 1) & (key_ids < total_len)
    tiles = GRID // 8
    query_t = query.reshape(tiles, 8, GRID, HEADS, HEAD_DIM)
    keys_t = keys.reshape(tiles, 8, GRID, HEADS, HEAD_DIM)
    values_t = values.reshape(tiles, 8, GRID, HEADS, HEAD_DIM)
    gate_t = gate.reshape(tiles, 8, GRID, HEADS, HEAD_DIM)
    row_ids = key_ids.reshape(tiles, 8)

    def one_tile(items):
        q_tile, k_tile, v_tile, g_tile, ids = items
        scores = jnp.einsum('bjhd,bkhd->bhjk', q_tile.astype(jnp.float32), k_tile.astype(jnp.float32), precision=lax.Precision.HIGHEST) + bias[None]
        scores = jnp.where(key_live[None, None, None, :], scores, -1000000000.0)
        top = lax.optimization_barrier(jnp.max(scores, axis=-1, keepdims=True))
        expo = jnp.exp(scores - top)
        total_w = lax.optimization_barrier(jnp.sum(expo, axis=-1))
        weights = expo.astype(jnp.bfloat16)
        attended = jnp.einsum('bhjk,bkhd->bjhd', weights.astype(jnp.float32), v_tile.astype(jnp.float32), precision=lax.Precision.HIGHEST)
        attended = attended / jnp.transpose(total_w, (0, 2, 1))[..., None]
        gated = g_tile * attended
        gated = jnp.where((ids < total_len)[:, None, None, None], gated, 0.0).astype(jnp.bfloat16)
        mixed = jnp.dot(gated.reshape(8 * GRID, HD), w_out, preferred_element_type=jnp.float32)
        return mixed.astype(jnp.bfloat16).reshape(8, GRID, C)
    update = lax.map(one_tile, (query_t, keys_t, values_t, gate_t, row_ids))
    return update.reshape(GRID, GRID, C)
```

```python
import functools
import math

import jax
import jax.numpy as jnp
from jax import lax
from jax.experimental import pallas as pl
from jax.experimental.pallas import tpu as pltpu
from jax.sharding import PartitionSpec as P

NT = (((1,), (1,)), ((), ()))


def layer_norm(block, gain):
    values = block.astype(jnp.float32)
    centre = values - jnp.mean(values, axis=-1, keepdims=True)
    spread = jnp.mean(centre * centre, axis=-1, keepdims=True)
    return (centre * lax.rsqrt(spread + 1e-05) * gain).astype(jnp.bfloat16)


def bias_kernel(pair_ref, gain_ref, w_ref, out_ref):
    heads = out_ref.shape[0]
    for row in range(pair_ref.shape[0]):
        normed = layer_norm(pair_ref[row], gain_ref[...])
        plane = lax.dot_general(w_ref[...], normed, NT, preferred_element_type=jnp.float32)
        out_ref[:, row, :] = plane[:heads]


def pair_bias(pair, gain, w_bias):
    rows, cols, width = pair.shape
    heads = w_bias.shape[1]
    padded = jnp.zeros((8 * pl.cdiv(heads, 8), width), jnp.bfloat16)
    padded = lax.dynamic_update_slice(padded, w_bias.T, (0, 0))
    step = 8
    return pl.pallas_call(
        bias_kernel,
        grid=(rows // step,),
        in_specs=[
            pl.BlockSpec((step, cols, width), lambda i: (i, 0, 0)),
            pl.BlockSpec((1, width), lambda i: (0, 0)),
            pl.BlockSpec(padded.shape, lambda i: (0, 0)),
        ],
        out_specs=pl.BlockSpec((heads, step, cols), lambda i: (0, i, 0)),
        out_shape=jax.ShapeDtypeStruct((heads, rows, cols), jnp.float32),
        cost_estimate=pl.CostEstimate(
            flops=2 * rows * cols * width * 8, bytes_accessed=rows * cols * width * 2, transcendentals=0
        ),
    )(pair, gain, padded)


def attend_kernel(blocks, heads, tile, info_ref, *refs):
    pair_refs = refs[:blocks]
    gain_ref, w_in_ref, gate_bias_ref, w_out_ref, bias_ref, live_ref = refs[blocks : blocks + 6]
    rest = refs[blocks + 6 :]
    out_refs, (bias_all, query_all, keys_all, values_all, gate_all, update_all) = rest[:-6], rest[-6:]
    span, width = keys_all.shape
    cols = pair_refs[0].shape[1]
    head_size = width // heads
    col_pos, place, total_len = info_ref[0], info_ref[1], info_ref[3]
    row_id = info_ref[2] + pl.program_id(0)
    scale = 1.0 / math.sqrt(head_size)

    @pl.when(pl.program_id(0) == 0)
    def _():
        live = live_ref[...] > 0
        for head in range(heads):

            @pl.loop(0, span // 64)
            def _(part):
                rows = pl.ds(pl.multiple_of(part * 64, 64), 64)
                bias_all[head, rows, :] = jnp.where(
                    live, bias_ref[head, rows, :].astype(jnp.float32), -1000000000.0
                )

        values_all[:, width:] = jnp.ones((span, width), jnp.bfloat16)

    for step in range(blocks):
        normed = layer_norm(pair_refs[step][0], gain_ref[...])
        start = jnp.bitwise_xor(col_pos, step) * cols
        rows = pl.ds(pl.multiple_of(start, 32), cols)
        mixed = jnp.dot(normed, w_in_ref[...], preferred_element_type=jnp.float32)
        query_all[rows, :] = (mixed[:, :width] * scale).astype(jnp.bfloat16)
        keys_all[rows, :] = mixed[:, width : 2 * width].astype(jnp.bfloat16)
        values_all[rows, :width] = mixed[:, 2 * width : 3 * width].astype(jnp.bfloat16)
        gate_all[rows, :] = jax.nn.sigmoid(mixed[:, 3 * width :] + gate_bias_ref[...])

    lanes = lax.broadcasted_iota(jnp.int32, (1, width), 1) // head_size
    row_scale = (row_id < total_len).astype(jnp.float32)

    @pl.loop(0, span // tile)
    def _(index):
        rows = pl.ds(pl.multiple_of(index * tile, tile), tile)
        query = query_all[rows, :]
        attended = jnp.zeros((tile, width), jnp.float32)
        for head in range(heads):
            masked = jnp.where(lanes == head, query, jnp.zeros_like(query))
            scores = lax.dot_general(masked, keys_all[...], NT, preferred_element_type=jnp.float32)
            scores = scores + bias_all[head, rows, :]
            top = jnp.max(scores, axis=-1, keepdims=True)
            weights = jnp.exp(scores - top).astype(jnp.bfloat16)
            summed = jnp.dot(weights, values_all[...], preferred_element_type=jnp.float32)
            attended = jnp.where(lanes == head, summed[:, :width] / summed[:, width:], attended)
        gated = gate_all[rows, :] * attended
        gated = jnp.where(row_scale > 0.0, gated, 0.0).astype(jnp.bfloat16)
        update = jnp.dot(gated, w_out_ref[...], preferred_element_type=jnp.float32)
        update_all[rows, :] = update.astype(jnp.bfloat16)

    half = out_refs[0].shape[1]
    for step in range(len(out_refs)):
        start = jnp.bitwise_xor(place, step) * half
        out_refs[step][0] = update_all[pl.ds(pl.multiple_of(start, 16), half), :]


def attend(parts, outs, info, gain, w_in, gate_bias, w_out, bias, live):
    rows, cols, width = parts[0].shape
    heads, span = bias.shape[0], bias.shape[1]
    half = span // outs
    tile = 256 if span % 256 == 0 else span
    whole = lambda array: pl.BlockSpec(
        array.shape, lambda i, *_, nd=array.ndim: (0,) * nd, pipeline_mode=pl.Buffered(1)
    )
    shared = (gain, w_in, gate_bias, w_out, bias, live)
    grid_spec = pltpu.PrefetchScalarGridSpec(
        num_scalar_prefetch=1,
        grid=(rows,),
        in_specs=[pl.BlockSpec((1, cols, width), lambda i, *_: (i, 0, 0)) for _ in parts]
        + [whole(array) for array in shared],
        out_specs=[pl.BlockSpec((1, half, width), lambda i, *_: (i, 0, 0)) for _ in range(outs)],
        scratch_shapes=[
            pltpu.VMEM((heads, span, span), jnp.float32),
            pltpu.VMEM((span, width), jnp.bfloat16),
            pltpu.VMEM((span, width), jnp.bfloat16),
            pltpu.VMEM((span, 2 * width), jnp.bfloat16),
            pltpu.VMEM((span, width), jnp.float32),
            pltpu.VMEM((span, width), jnp.bfloat16),
        ],
    )
    return pl.pallas_call(
        functools.partial(attend_kernel, len(parts), heads, tile),
        grid_spec=grid_spec,
        out_shape=[jax.ShapeDtypeStruct((rows, half, width), jnp.bfloat16) for _ in range(outs)],
        compiler_params=pltpu.CompilerParams(vmem_limit_bytes=48 * 1024 * 1024),
        cost_estimate=pl.CostEstimate(
            flops=rows * heads * span * span * 256 * 4,
            bytes_accessed=rows * span * width * 4,
            transcendentals=rows * heads * span * span,
        ),
    )(info, *parts, *shared)


def per_device(
    n_col,
    n_head,
    pair,
    crop_length,
    residue_mask,
    ln_gain,
    w_query,
    w_key,
    w_value,
    w_gate,
    gate_bias,
    w_bias,
    w_out,
):
    rows_here, cols_here, width = pair.shape
    grid_len = residue_mask.shape[0]
    row_pos = lax.axis_index("row")
    col_pos = lax.axis_index("col")
    head_pos = lax.axis_index("head")
    places = n_col * n_head
    place = col_pos * n_head + head_pos
    own_rows = rows_here // places
    chunk = 8 if own_rows % 8 == 0 else own_rows
    chunks = own_rows // chunk

    def rows_of(target, index):
        start = (target * n_head + head_pos) * own_rows + index * chunk
        return lax.dynamic_slice_in_dim(pair, start, chunk, 0)

    arrived = []
    for index in range(chunks):
        parts = [rows_of(col_pos, index)]
        for step in range(1, n_col):
            swap = [(d, d ^ step) for d in range(n_col)]
            parts.append(lax.ppermute(rows_of(col_pos ^ step, index), "col", swap))
        arrived.append(parts)

    local_chan = w_query.shape[1]
    local_heads = w_bias.shape[1]
    gain = ln_gain.reshape(1, width)
    w_bias_all = lax.all_gather(w_bias.T, "head", axis=0, tiled=True).T
    weights = jnp.concatenate([w_query, w_key, w_value, w_gate], axis=1).astype(jnp.float32)
    extra = jnp.zeros((8, weights.shape[1]), jnp.float32)
    extra = lax.dynamic_update_slice(extra, gate_bias[None], (0, 0))
    packed = lax.all_gather(jnp.concatenate([weights, extra], axis=0), "head", axis=0)
    w_in = packed[:, :width].reshape(n_head, width, 4, local_chan)
    w_in = jnp.transpose(w_in, (1, 2, 0, 3)).reshape(width, -1).astype(jnp.bfloat16)
    gate_bias_all = packed[:, width, :local_chan].reshape(1, -1)

    bias_rows = rows_here // n_head
    bias = pair_bias(
        lax.dynamic_slice_in_dim(pair, head_pos * bias_rows, bias_rows, 0), gain, w_bias_all
    ).astype(jnp.bfloat16)
    bias = lax.all_gather(bias, "col", axis=2, tiled=True)
    bias = lax.all_gather(bias, ("row", "head"), axis=1, tiled=True)

    total_len = crop_length[0]
    key_ids = jnp.arange(grid_len, dtype=jnp.int32)
    live = ((residue_mask == 1) & (key_ids < total_len)).astype(jnp.int32).reshape(1, grid_len)

    update = jnp.zeros((places, own_rows, cols_here // n_head, width), jnp.bfloat16)
    for index in range(chunks):
        first_row = row_pos * rows_here + place * own_rows + index * chunk
        info = jnp.stack([col_pos, place, first_row, total_len]).astype(jnp.int32)
        outs = attend(arrived[index], places, info, gain, w_in, gate_bias_all, w_out, bias, live)
        for step in range(places):
            got = outs[step]
            if step > 0:
                swap = [(d, d ^ step) for d in range(places)]
                got = lax.ppermute(got, ("col", "head"), swap)
            update = lax.dynamic_update_slice(
                update, got[None], (place ^ step, index * chunk, 0, 0)
            )
    return update.reshape(rows_here, cols_here // n_head, width)


def solution(mesh):
    placed = (
        P(("parts", "row"), "col", None),
        P("parts"),
        P("parts"),
        P(),
        P(None, "head"),
        P(None, "head"),
        P(None, "head"),
        P(None, "head"),
        P("head"),
        P(None, "head"),
        P(),
    )
    return jax.shard_map(
        functools.partial(per_device, mesh.shape["col"], mesh.shape["head"]),
        mesh=mesh,
        in_specs=placed,
        out_specs=P(("parts", "row"), ("col", "head"), None),
        check_vma=False,
    )
```

```python
import functools
import math

import jax
import jax.numpy as jnp
from jax import lax
from jax.experimental import pallas as pl
from jax.experimental.pallas import tpu as pltpu
from jax.sharding import PartitionSpec as P

NT = (((1,), (1,)), ((), ()))


def layer_norm(block, gain):
    values = block.astype(jnp.float32)
    centre = values - jnp.mean(values, axis=-1, keepdims=True)
    spread = jnp.mean(centre * centre, axis=-1, keepdims=True)
    return (centre * lax.rsqrt(spread + 1e-05) * gain).astype(jnp.bfloat16)


def bias_kernel(first_ref, pair_ref, gain_ref, w_ref, out_ref):
    heads = out_ref.shape[0]
    for row in range(pair_ref.shape[0]):
        normed = layer_norm(pair_ref[row], gain_ref[...])
        plane = lax.dot_general(w_ref[...], normed, NT, preferred_element_type=jnp.float32)
        out_ref[:, row, :] = plane[:heads]


def pair_bias(pair, first, rows, gain, w_bias):
    cols, width = pair.shape[1:]
    heads = w_bias.shape[1]
    padded = jnp.zeros((8 * pl.cdiv(heads, 8), width), jnp.bfloat16)
    padded = lax.dynamic_update_slice(padded, w_bias.T, (0, 0))
    step = 8
    return pl.pallas_call(
        bias_kernel,
        grid_spec=pltpu.PrefetchScalarGridSpec(
            num_scalar_prefetch=1,
            grid=(rows // step,),
            in_specs=[
                pl.BlockSpec((step, cols, width), lambda i, first: (first[0] + i, 0, 0)),
                pl.BlockSpec((1, width), lambda i, first: (0, 0)),
                pl.BlockSpec(padded.shape, lambda i, first: (0, 0)),
            ],
            out_specs=pl.BlockSpec((heads, step, cols), lambda i, first: (0, i, 0)),
        ),
        out_shape=jax.ShapeDtypeStruct((heads, rows, cols), jnp.float32),
        cost_estimate=pl.CostEstimate(
            flops=2 * rows * cols * width * 8, bytes_accessed=rows * cols * width * 2, transcendentals=0
        ),
    )((first // step).reshape(1).astype(jnp.int32), pair, gain, padded)


def attend_kernel(blocks, heads, tile, info_ref, *refs):
    pair_refs = refs[:blocks]
    gain_ref, w_in_ref, gate_bias_ref, w_out_ref, bias_ref = refs[blocks : blocks + 5]
    rest = refs[blocks + 5 :]
    out_refs, scratch = rest[:-6], rest[-6:]
    query_all, keys_all, keys_turned, values_all, gate_all, update_all = scratch
    span, width = keys_all.shape
    cols = pair_refs[0].shape[1]
    head_size = width // heads
    col_pos, place, total_len = info_ref[0], info_ref[1], info_ref[3]
    row_id = info_ref[2] + pl.program_id(0)
    scale = 1.0 / math.sqrt(head_size)

    @pl.when(pl.program_id(0) == 0)
    def _():
        values_all[:, width:] = jnp.ones((span, width), jnp.bfloat16)

    for step in range(blocks):
        normed = layer_norm(pair_refs[step][0], gain_ref[...])
        start = jnp.bitwise_xor(col_pos, step) * cols
        rows = pl.ds(pl.multiple_of(start, 32), cols)
        mixed = jnp.dot(normed, w_in_ref[...], preferred_element_type=jnp.float32)
        query_all[rows, :] = (mixed[:, :width] * scale).astype(jnp.bfloat16)
        keys_all[rows, :] = mixed[:, width : 2 * width].astype(jnp.bfloat16)
        values_all[rows, :width] = mixed[:, 2 * width : 3 * width].astype(jnp.bfloat16)
        gate_all[rows, :] = jax.nn.sigmoid(mixed[:, 3 * width :] + gate_bias_ref[...])

    keys_turned[...] = keys_all[...].T
    lanes = lax.broadcasted_iota(jnp.int32, (1, width), 1) // head_size
    row_scale = (row_id < total_len).astype(jnp.float32)

    @pl.loop(0, span // tile)
    def _(index):
        rows = pl.ds(pl.multiple_of(index * tile, tile), tile)
        query = query_all[rows, :]
        attended = jnp.zeros((tile, width), jnp.float32)
        for head in range(heads):
            masked = jnp.where(lanes == head, query, jnp.zeros_like(query))
            scores = jnp.dot(masked, keys_turned[...], preferred_element_type=jnp.float32)
            scores = scores + bias_ref[head, rows, :].astype(jnp.float32)
            top = jnp.max(scores, axis=-1, keepdims=True)
            weights = jnp.exp(scores - top).astype(jnp.bfloat16)
            summed = jnp.dot(weights, values_all[...], preferred_element_type=jnp.float32)
            attended = jnp.where(lanes == head, summed[:, :width] / summed[:, width:], attended)
        gated = gate_all[rows, :] * attended
        gated = jnp.where(row_scale > 0.0, gated, 0.0).astype(jnp.bfloat16)
        update = jnp.dot(gated, w_out_ref[...], preferred_element_type=jnp.float32)
        update_all[rows, :] = update.astype(jnp.bfloat16)

    half = out_refs[0].shape[1]
    for step in range(len(out_refs)):
        start = jnp.bitwise_xor(place, step) * half
        out_refs[step][0] = update_all[pl.ds(pl.multiple_of(start, 16), half), :]


def attend(parts, outs, info, gain, w_in, gate_bias, w_out, bias):
    rows, cols, width = parts[0].shape
    heads, span = bias.shape[0], bias.shape[1]
    half = span // outs
    tile = span
    whole = lambda array: pl.BlockSpec(
        array.shape, lambda i, *_, nd=array.ndim: (0,) * nd, pipeline_mode=pl.Buffered(1)
    )
    shared = (gain, w_in, gate_bias, w_out, bias)
    grid_spec = pltpu.PrefetchScalarGridSpec(
        num_scalar_prefetch=1,
        grid=(rows,),
        in_specs=[pl.BlockSpec((1, cols, width), lambda i, *_: (i, 0, 0)) for _ in parts]
        + [whole(array) for array in shared],
        out_specs=[pl.BlockSpec((1, half, width), lambda i, *_: (i, 0, 0)) for _ in range(outs)],
        scratch_shapes=[
            pltpu.VMEM((span, width), jnp.bfloat16),
            pltpu.VMEM((span, width), jnp.bfloat16),
            pltpu.VMEM((width, span), jnp.bfloat16),
            pltpu.VMEM((span, 2 * width), jnp.bfloat16),
            pltpu.VMEM((span, width), jnp.float32),
            pltpu.VMEM((span, width), jnp.bfloat16),
        ],
    )
    return pl.pallas_call(
        functools.partial(attend_kernel, len(parts), heads, tile),
        grid_spec=grid_spec,
        out_shape=[jax.ShapeDtypeStruct((rows, half, width), jnp.bfloat16) for _ in range(outs)],
        compiler_params=pltpu.CompilerParams(vmem_limit_bytes=48 * 1024 * 1024),
        cost_estimate=pl.CostEstimate(
            flops=rows * heads * span * span * 256 * 4,
            bytes_accessed=rows * span * width * 4,
            transcendentals=rows * heads * span * span,
        ),
    )(info, *parts, *shared)


def per_device(
    n_col,
    n_head,
    pair,
    crop_length,
    residue_mask,
    ln_gain,
    w_query,
    w_key,
    w_value,
    w_gate,
    gate_bias,
    w_bias,
    w_out,
):
    rows_here, cols_here, width = pair.shape
    grid_len = residue_mask.shape[0]
    row_pos = lax.axis_index("row")
    col_pos = lax.axis_index("col")
    head_pos = lax.axis_index("head")
    places = n_col * n_head
    place = col_pos * n_head + head_pos
    own_rows = rows_here // places
    chunk = 8 if own_rows % 8 == 0 else own_rows
    chunks = own_rows // chunk

    def rows_of(target, index):
        start = (target * n_head + head_pos) * own_rows + index * chunk
        return lax.dynamic_slice_in_dim(pair, start, chunk, 0)

    first_parts = [
        [rows_of(col_pos ^ step, index) for step in range(n_col)] for index in range(min(chunks, 2))
    ]
    local_chan = w_query.shape[1]
    local_heads = w_bias.shape[1]
    gain = ln_gain.reshape(1, width)
    w_bias_all = lax.all_gather(w_bias.T, "head", axis=0, tiled=True).T
    weights = jnp.concatenate([w_query, w_key, w_value, w_gate], axis=1).astype(jnp.float32)
    extra = jnp.zeros((8, weights.shape[1]), jnp.float32)
    extra = lax.dynamic_update_slice(extra, gate_bias[None], (0, 0))
    packed = lax.all_gather(jnp.concatenate([weights, extra], axis=0), "head", axis=0)
    w_in = packed[:, :width].reshape(n_head, width, 4, local_chan)
    w_in = jnp.transpose(w_in, (1, 2, 0, 3)).reshape(width, -1).astype(jnp.bfloat16)
    gate_bias_all = packed[:, width, :local_chan].reshape(1, -1)

    bias_rows = rows_here // n_head
    first_row = head_pos * bias_rows
    first_row, first_parts = lax.optimization_barrier((first_row, first_parts))
    bias = pair_bias(pair, first_row, bias_rows, gain, w_bias_all)
    arrived = []
    for index in range(chunks):
        if index < len(first_parts):
            parts = first_parts[index]
        else:
            parts = [rows_of(col_pos ^ step, index) for step in range(n_col)]
        for step in range(1, n_col):
            swap = [(d, d ^ step) for d in range(n_col)]
            parts[step] = lax.ppermute(parts[step], "col", swap)
        arrived.append(parts)
    bias = lax.all_gather(bias.astype(jnp.bfloat16), "col", axis=2, tiled=True)
    bias, arrived[0] = lax.optimization_barrier((bias, arrived[0]))
    bias = lax.all_gather(bias, ("row", "head"), axis=1, tiled=True)
    for index in range(1, min(chunks, 2)):
        bias, arrived[index] = lax.optimization_barrier((bias, arrived[index]))
    total_len = crop_length[0]
    key_ids = jnp.arange(grid_len, dtype=jnp.int32)
    live = (residue_mask == 1) & (key_ids < total_len)
    bias = jnp.where(live[None, None], bias, jnp.bfloat16(-1e9))

    update = jnp.zeros((places, own_rows, cols_here // n_head, width), jnp.bfloat16)
    sent = [()] * chunks
    for index in range(chunks):
        first_row = row_pos * rows_here + place * own_rows + index * chunk
        info = jnp.stack([col_pos, place, first_row, total_len]).astype(jnp.int32)
        if index == 1:
            info, arrived[2:] = lax.optimization_barrier((info, arrived[2:]))
        if index >= 2:
            info, sent[index - 2] = lax.optimization_barrier((info, sent[index - 2]))
        outs = attend(arrived[index], places, info, gain, w_in, gate_bias_all, w_out, bias)
        got = [outs[0]]
        for step in range(1, places):
            swap = [(d, d ^ step) for d in range(places)]
            got.append(lax.ppermute(outs[step], ("col", "head"), swap))
        sent[index] = tuple(got)
    for index in range(chunks):
        for step in range(places):
            update = lax.dynamic_update_slice(
                update, sent[index][step][None], (place ^ step, index * chunk, 0, 0)
            )
    return update.reshape(rows_here, cols_here // n_head, width)


def solution(mesh):
    placed = (
        P(("parts", "row"), "col", None),
        P("parts"),
        P("parts"),
        P(),
        P(None, "head"),
        P(None, "head"),
        P(None, "head"),
        P(None, "head"),
        P("head"),
        P(None, "head"),
        P(),
    )
    return jax.shard_map(
        functools.partial(per_device, mesh.shape["col"], mesh.shape["head"]),
        mesh=mesh,
        in_specs=placed,
        out_specs=P(("parts", "row"), ("col", "head"), None),
        check_vma=False,
    )
```
